128 devices in a mesh: dp: 8 (over x, core), expert: 16 (over z, y).
Axes of the slice: x: 4, y: 4, z: 4, core: 2. Of those that a mesh axis runs over, the one named last changes fastest.
Arguments:
- tokens: bfloat16 [16384, 4096], P(('dp', 'expert')), may hold values from -6 to 6
- norm_gain: float32 [4096], replicated, may hold values from 0.1 to 1.9
- routes: int32 [16384, 1], P(('dp', 'expert')), may hold values from 0 to 7; in each aligned block of 128 rows (0 to 127, 128 to 255, ...) at most 16 rows name the same one
- route_weight: float32 [16384, 1], P(('dp', 'expert')), may hold values from 0.2 to 1
- gate_weight: bfloat16 [8, 1536, 4096], P('dp', 'expert'), may hold values from -0.09375 to 0.09375
- up_weight: bfloat16 [8, 1536, 4096], P('dp', 'expert'), may hold values from -0.09375 to 0.09375
- down_weight: bfloat16 [8, 1536, 4096], P('dp', 'expert'), may hold values from -0.15625 to 0.15625
- cotangent: bfloat16 [16384, 4096], P(('dp', 'expert')), may hold values from -6 to 6
Outputs:
- grad_tokens: bfloat16 [16384, 4096], P(('dp', 'expert'))
- grad_gate: bfloat16 [8, 1536, 4096], P('dp', 'expert')
- grad_up: bfloat16 [8, 1536, 4096], P('dp', 'expert')
- grad_down: bfloat16 [8, 1536, 4096], P('dp', 'expert')
The draws below stay inside these ranges and needn't reach their ends.
Inputs may be any that keep to these rules, and one draw needn't show every extreme that they name: `routes`: among the tokens of one device exactly 16 have each expert.
All inputs are finite; a program needn't handle non-finite values.
Results may differ from the reference program's by a relative error of at most 0.013.
Values may be sent and summed in bfloat16 or wider, within the bound.
A program may use at most 192 MiB of HBM per device.

```python
import math
import jax
import jax.numpy as jnp
import numpy as np
from jax import lax

D = 4096
FF = 1536
TOK_DEV = 128
EXPERTS = 8
CAP = 16
TOKENS = 16384
N_DP = 8
N_EXPERT = 16


def levels(key, dims, pieces, smallest, high):
    level = 1.0
    for dim, parts in pieces:
        heights = jax.random.uniform(jax.random.fold_in(jax.random.fold_in(key, 6), dim), (parts,), jnp.float32, smallest / len(pieces), high / len(pieces))
        level = level * jnp.repeat(jnp.exp(heights), dims[dim] // parts).reshape((-1,) + (1,) * (len(dims) - 1 - dim))
    return level


def shared_out(rng, own, number, rows, amount, top, bound, skew):
    ranking = jax.random.permutation(rng, amount)
    crowded, usual = load_shares(amount, rows * top, bound, skew, True), load_shares(amount, rows * top, bound, skew, False)
    places = jnp.arange(amount)

    def named(lengths, turn):
        used = int((lengths > 0).sum())
        fixed = max(1, used // 4)
        shifted = fixed + (places - fixed + turn * (used - fixed)) % max(1, amount - fixed)
        return jnp.zeros((amount,), jnp.int32).at[ranking[jnp.where(places < fixed, places, shifted)]].set(jnp.asarray(lengths, jnp.int32))

    lengths = jnp.where(number % 4 == 0, named(crowded, number // 4), named(usual, number - number // 4 - 1))
    mixed = jax.random.permutation(jax.random.fold_in(own, 3), amount)
    source_of, receiver = mixed[0:amount // 2 * 2:2], mixed[1:amount // 2 * 2:2]
    slack = jnp.minimum(lengths[source_of] - 1, bound - lengths[receiver]) // 2
    slack = jnp.where((source_of == ranking[0]) | (receiver == ranking[0]) | (lengths[receiver] == 0), 0, jnp.maximum(slack, 0))
    shifted = jax.random.randint(jax.random.fold_in(own, 4), (amount // 2,), 0, 1 << 20) % (slack + 1)
    lengths = lengths.at[source_of].add(-shifted).at[receiver].add(shifted)
    labels = jnp.searchsorted(jnp.cumsum(lengths), jnp.arange(rows * top), side="right").astype(jnp.int32)
    table = labels.reshape(top, rows).T
    table = table[jax.random.permutation(jax.random.fold_in(own, 1), rows)]
    turn = jax.random.randint(jax.random.fold_in(own, 2), (rows, 1), 0, top)
    return jnp.take_along_axis(table, (jnp.arange(top)[None, :] + turn) % top, axis=1)


def load_shares(count, total, limit, skew, full):
    portions = [(1 << 20) // math.isqrt(rank ** skew) + 1 for rank in range(1, count + 1)]
    largest = limit if full else min(limit, max(-(-total // count), total * portions[0] // sum(portions)))
    least = 1 if total - largest >= count - 1 else 0
    holding, spare = [largest] + [least] * (count - 1), total - largest - least * (count - 1)
    while spare > 0:
        movable = [i for i in range(1, count) if holding[i] < largest] or [i for i in range(1, count) if holding[i] < limit]
        pool, remaining = sum([portions[i] for i in movable]), spare
        for i in movable:
            more = min(limit - holding[i], max(1, remaining * portions[i] // pool), spare)
            holding[i] = holding[i] + more
            spare = spare - more
    return np.array(holding)


def noise(own_key, extent, width, bound, shards=(), kind=jnp.bfloat16):
    factor_of = levels(own_key, extent, shards, -0.22, 0.18) if shards else 1.0
    array = jax.random.normal(own_key, extent, jnp.float32) * width * factor_of
    return jnp.minimum(jnp.maximum(array, -bound), bound).astype(kind)


def setup_inputs(seed: int = 0) -> dict:
    splits = jax.random.split(jax.random.key(seed), 9)
    tokens = noise(splits[0], (TOKENS, D), 1.0, 6.0, ((0, 128),))
    norm_gain = jnp.clip(1.0 + 0.18 * jax.random.normal(splits[1], (D,), jnp.float32), 0.1, 1.9)
    routes_keys = jax.random.split(jax.random.fold_in(splits[2], 1), TOKENS // TOK_DEV)
    routes_turns = jax.random.permutation(jax.random.fold_in(splits[2], 3), TOKENS // TOK_DEV)
    routes = jax.vmap(lambda own, number: shared_out(jax.random.fold_in(splits[2], 2), own, number, TOK_DEV, EXPERTS, 1, CAP, 0))(routes_keys, routes_turns).reshape((TOKENS, 1))
    route_weight = jnp.clip(0.2 + 0.8 * jax.random.uniform(splits[3], (TOKENS, 1), jnp.float32) ** levels(splits[3], (TOKENS, 1), ((0, 128),), -0.2, 0.2), 0.2, 1.0)
    gate_weight = noise(splits[4], (EXPERTS, FF, D), D ** -0.5, 0.09375, ((0, 8), (1, 16)))
    up_weight = noise(splits[5], (EXPERTS, FF, D), D ** -0.5, 0.09375, ((0, 8), (1, 16)))
    down_weight = noise(splits[6], (EXPERTS, FF, D), FF ** -0.5, 0.15625, ((0, 8), (1, 16)))
    cotangent = noise(splits[7], (TOKENS, D), 1.0, 6.0, ((0, 128),))
    return dict(tokens=tokens, norm_gain=norm_gain, routes=routes, route_weight=route_weight, gate_weight=gate_weight, up_weight=up_weight, down_weight=down_weight, cotangent=cotangent)


def slot_layout(routes):
    devices = N_DP * N_EXPERT
    chosen = routes[:, 0].reshape(devices, TOK_DEV).astype(jnp.int32)
    onehot = (chosen[:, :, None] == jnp.arange(EXPERTS, dtype=jnp.int32)[None, None, :]).astype(jnp.int32)
    earlier = jnp.cumsum(onehot, axis=1) - onehot
    position = lax.optimization_barrier(jnp.sum(earlier * onehot, axis=2)).astype(jnp.int32)
    source = jnp.broadcast_to(jnp.arange(devices, dtype=jnp.int32)[:, None], (devices, TOK_DEV))
    return (chosen, source, position)

def block_sum(left, right):
    slices = FF // N_EXPERT
    left_blocks = left.astype(jnp.float32).reshape(N_EXPERT, slices, left.shape[1])
    right_blocks = right.astype(jnp.float32).reshape(N_EXPERT, slices, D)
    return jnp.einsum('sfr,sfd->srd', left_blocks, right_blocks)

def expert_pass(operands):
    rows, row_grads, gate_mat, up_mat, down_mat = operands
    gate_pre = jnp.dot(gate_mat, rows.T, preferred_element_type=jnp.float32)
    up_pre = jnp.dot(up_mat, rows.T, preferred_element_type=jnp.float32)
    sigmoid_gate = jax.nn.sigmoid(gate_pre)
    active = gate_pre * sigmoid_gate
    hidden = (active * up_pre).astype(jnp.bfloat16)
    hidden_grad = jnp.dot(down_mat, row_grads.T, preferred_element_type=jnp.float32)
    gate_act = (hidden_grad * up_pre * sigmoid_gate * (1.0 + gate_pre * (1.0 - sigmoid_gate))).astype(jnp.bfloat16)
    up_act = (hidden_grad * active).astype(jnp.bfloat16)
    grad_gate = jnp.dot(gate_act, rows, preferred_element_type=jnp.float32).astype(jnp.bfloat16)
    grad_up = jnp.dot(up_act, rows, preferred_element_type=jnp.float32).astype(jnp.bfloat16)
    grad_down = jnp.dot(hidden, row_grads, preferred_element_type=jnp.float32).astype(jnp.bfloat16)
    partial_in = block_sum(gate_act, gate_mat) + block_sum(up_act, up_mat)
    partial_in = lax.optimization_barrier(partial_in.astype(jnp.bfloat16))
    normed_grad = lax.optimization_barrier(jnp.sum(partial_in.astype(jnp.float32), axis=0)).astype(jnp.bfloat16)
    return (normed_grad, grad_gate, grad_up, grad_down)

def reference(tokens, norm_gain, routes, route_weight, gate_weight, up_weight, down_weight, cotangent):
    devices = N_DP * N_EXPERT
    tokens_float = tokens.astype(jnp.float32)
    inv_rms = lax.rsqrt(lax.optimization_barrier(jnp.mean(tokens_float * tokens_float, axis=-1, keepdims=True)) + 1e-06)
    unit_rows = tokens_float * inv_rms
    normed = (unit_rows * norm_gain).astype(jnp.bfloat16)
    row_grad = (route_weight * cotangent.astype(jnp.float32)).astype(jnp.bfloat16)
    chosen, source, position = slot_layout(routes)
    empty = jnp.zeros((EXPERTS, devices, CAP, D), jnp.bfloat16)
    rows_all = empty.at[chosen, source, position].set(normed.reshape(devices, TOK_DEV, D))
    grads_all = empty.at[chosen, source, position].set(row_grad.reshape(devices, TOK_DEV, D))
    results = lax.map(expert_pass, (rows_all.reshape(EXPERTS, devices * CAP, D), grads_all.reshape(EXPERTS, devices * CAP, D), gate_weight, up_weight, down_weight))
    normed_grad, grad_gate, grad_up, grad_down = results
    back_grad = normed_grad.reshape(EXPERTS, devices, CAP, D)[chosen, source, position].reshape(TOKENS, D)
    scaled_grad = back_grad.astype(jnp.float32) * norm_gain
    moved = inv_rms * (scaled_grad - unit_rows * lax.optimization_barrier(jnp.mean(scaled_grad * unit_rows, axis=-1, keepdims=True)))
    grad_tokens = (cotangent.astype(jnp.float32) + moved).astype(jnp.bfloat16)
    return (grad_tokens, grad_gate, grad_up, grad_down)
```

```python
import functools

import jax
import jax.numpy as jnp
from jax import lax
from jax.experimental import pallas as pl
from jax.experimental.pallas import tpu as pltpu
from jax.sharding import PartitionSpec as P

MESH = pl.DeviceIdType.MESH
F32, BF16 = jnp.float32, jnp.bfloat16
D = 4096
TOK = 128
CAP = 16
HID = 96
HALF = 64
COLS = 512
SLOTS = 4

N_REMOTE = 80
N_LOCAL = 16


def dot(left, right, left_dim, right_dim):
    return lax.dot_general(
        left, right, (((left_dim,), (right_dim,)), ((), ())), preferred_element_type=F32
    )


def kernel(
    tok_hbm, cot_hbm, gain_ref, routes_ref, rw_ref, gate_hbm, up_hbm, down_hbm,
    gt_hbm, gg_hbm, gu_hbm, gd_hbm,
    tok, cot, norm, rgrad, send_n, send_g, place, inv,
    rn, rg, wgu, wd, pre, hg, act, act_t, hid,
    part, ptl, ptr, pfl, pfr, ret_send, ret, qbuf, out_t,
    pg, pd, gtl, gtr, gfl, gfr,
    ssem, rsem, lsem,
):
    dp = lax.axis_index("dp")
    ex = lax.axis_index("expert")
    core = lax.rem(dp, 2)
    rstride = 1 + 3 * core
    wstride = 4 - 3 * core
    rpos = lax.rem(lax.div(ex, rstride), 4)
    wpos = lax.rem(lax.div(ex, wstride), 4)
    r_right = (dp, ex + rstride * (lax.rem(rpos + 1, 4) - rpos))
    r_left = (dp, ex + rstride * (lax.rem(rpos + 3, 4) - rpos))
    w_right = (dp, ex + wstride * (lax.rem(wpos + 1, 4) - wpos))
    w_left = (dp, ex + wstride * (lax.rem(wpos + 3, 4) - wpos))

    count = [0, 0]
    sent = []

    def local(src, dst):
        copy = pltpu.make_async_copy(src, dst, lsem.at[count[1]])
        count[1] += 1
        copy.start()
        return copy

    def remote(src, dst, device):
        copy = pltpu.make_async_remote_copy(
            src_ref=src, dst_ref=dst, send_sem=ssem.at[count[0]], recv_sem=rsem.at[count[0]],
            device_id=device, device_id_type=MESH,
        )
        count[0] += 1
        copy.start()
        sent.append(copy)
        return copy

    tok_in = local(tok_hbm, tok)
    cot_in = local(cot_hbm, cot)

    barrier = pltpu.get_barrier_semaphore()
    partners = [r_right, r_left, w_right, w_left]
    partners += [(lax.rem(dp + k, 8), ex) for k in range(1, 8)]
    for device in partners:
        pl.semaphore_signal(barrier, inc=1, device_id=device, device_id_type=MESH)
    pl.semaphore_wait(barrier, len(partners))

    w_from_left, w_from_right = [], []
    places = [(gate_hbm, wgu, 192, 0), (up_hbm, wgu, 192, 96), (down_hbm, wd, 96, 0)]
    for src, buf, step, at in places:
        w_from_left.append(remote(src, buf.at[pl.ds(step + at, HID)], w_right))
        w_from_right.append(remote(src, buf.at[pl.ds(2 * step + at, HID)], w_left))
    w_own = [local(src, buf.at[pl.ds(at, HID)]) for src, buf, step, at in places]

    chosen = routes_ref[...]
    lane = lax.broadcasted_iota(jnp.int32, (TOK, TOK), 1)
    sub = lax.broadcasted_iota(jnp.int32, (TOK, TOK), 0)
    onehot = (chosen == lane).astype(F32)
    earlier = dot((lane < sub).astype(F32).astype(BF16), onehot.astype(BF16), 1, 0)
    position = jnp.sum(earlier * onehot, axis=1, keepdims=True)
    piece = jnp.bitwise_and(dp - chosen + 8, 7)
    slot = piece.astype(F32) * CAP + position
    place[...] = (slot == lane.astype(F32)).astype(F32).astype(BF16)

    tok_in.wait()
    cot_in.wait()

    def norm_rows(i, carry):
        rows = pl.ds(pl.multiple_of(i * 16, 16), 16)
        x = tok[rows, :].astype(F32)
        scale = lax.rsqrt(jnp.mean(x * x, axis=-1, keepdims=True) + 1e-06)
        inv[rows, :] = jnp.broadcast_to(scale, (16, 128))
        norm[rows, :] = ((x * scale) * gain_ref[...]).astype(BF16)
        rgrad[rows, :] = (rw_ref[rows, :] * cot[rows, :].astype(F32)).astype(BF16)
        return carry

    lax.fori_loop(0, TOK // 16, norm_rows, 0)

    placing_t = place[...].astype(F32).T.astype(BF16)

    def place_rows(i, carry):
        cols = pl.ds(pl.multiple_of(i * COLS, COLS), COLS)
        send_n[:, cols] = dot(placing_t, norm[:, cols], 1, 0).astype(BF16)
        send_g[:, cols] = dot(placing_t, rgrad[:, cols], 1, 0).astype(BF16)
        return carry

    lax.fori_loop(0, D // COLS, place_rows, 0)

    def at_piece(k):
        return pl.ds((k // 4) * 256 + (k % 4) * CAP, CAP)

    arrive = {0: [], 1: []}
    rn[at_piece(0), :] = send_n[pl.ds(0, CAP), :]
    rg[at_piece(0), :] = send_g[pl.ds(0, CAP), :]
    for k in range(1, 8):
        owner = (lax.rem(dp + 8 - k, 8), ex)
        piece_rows = pl.ds(k * CAP, CAP)
        arrive[k // 4].append(remote(send_n.at[piece_rows], rn.at[at_piece(k)], owner))
        arrive[k // 4].append(remote(send_g.at[piece_rows], rg.at[at_piece(k)], owner))

    w_from_left[0].wait_recv()
    w_last = [remote(wgu.at[pl.ds(192, HID)], wgu.at[pl.ds(3 * 192, HID)], w_right)]
    w_from_right[0].wait_recv()
    w_from_left[1].wait_recv()
    w_from_right[1].wait_recv()
    w_last.append(remote(wgu.at[pl.ds(2 * 192 + 96, HID)], wgu.at[pl.ds(3 * 192 + 96, HID)], w_left))
    w_from_left[2].wait_recv()
    w_last.append(remote(wd.at[pl.ds(HID, 48)], wd.at[pl.ds(3 * HID, 48)], w_right))
    w_from_right[2].wait_recv()
    w_last.append(remote(wd.at[pl.ds(2 * HID + 48, 48)], wd.at[pl.ds(3 * HID + 48, 48)], w_left))

    def row_slot(half, s, at=0, size=HALF):
        return pl.ds(half * 256 + s * HALF + at, size)

    def send_own(buf, half):
        return (
            remote(buf.at[row_slot(half, 0)], buf.at[row_slot(half, 1)], r_right),
            remote(buf.at[row_slot(half, 0)], buf.at[row_slot(half, 2)], r_left),
        )

    def pass_on(buf, half, first):
        first[0].wait_recv()
        a = remote(buf.at[row_slot(half, 1, 0, 32)], buf.at[row_slot(half, 3, 0, 32)], r_right)
        first[1].wait_recv()
        b = remote(buf.at[row_slot(half, 2, 32, 32)], buf.at[row_slot(half, 3, 32, 32)], r_left)
        return a, b

    for copy in arrive[0]:
        copy.wait_recv()
    own_an = send_own(rn, 0)
    own_ag = send_own(rg, 0)
    for copy in arrive[1]:
        copy.wait_recv()
    own_bn = send_own(rn, 1)
    last_a = [*pass_on(rn, 0, own_an), *pass_on(rg, 0, own_ag)]
    own_bg = send_own(rg, 1)
    last_b = [*pass_on(rn, 1, own_bn), *pass_on(rg, 1, own_bg)]

    for copy in (*w_own,):
        copy.wait()
    for copy in w_last:
        copy.wait_recv()

    def activations(half):
        rows = pl.ds(half * 256, 256)

        def per_slot(s, carry):
            two = pl.ds(pl.multiple_of(s * 192, 96), 192)
            one = pl.ds(pl.multiple_of(s * HID, HID), HID)
            pre[...] = dot(wgu[two, :], rn[rows, :], 1, 1)
            hidden_grad = dot(wd[one, :], rg[rows, :], 1, 1)
            gate = pre[pl.ds(0, HID), :]
            up = pre[pl.ds(HID, HID), :]
            sig = jax.nn.sigmoid(gate)
            active = gate * sig
            hid[one, rows] = (active * up).astype(BF16)
            act[pl.ds(pl.multiple_of(s * 192, 96), HID), rows] = (
                hidden_grad * up * sig * (1.0 + gate * (1.0 - sig))
            ).astype(BF16)
            act[pl.ds(pl.multiple_of(s * 192 + HID, 96), HID), rows] = (hidden_grad * active).astype(BF16)
            return carry

        lax.fori_loop(0, SLOTS, per_slot, 0)

    def partials(half):
        rows = pl.ds(half * 256, 256)
        act_t[...] = act[:, rows].astype(F32).T.astype(BF16)

        def per_cols(i, carry):
            cols = pl.ds(pl.multiple_of(i * COLS, COLS), COLS)
            part[rows, cols] = dot(act_t[...], wgu[:, cols], 1, 0).astype(BF16)
            return carry

        lax.fori_loop(0, D // COLS, per_cols, 0)

    def add_into(buf, start, other, at, size):
        def per_rows(i, carry):
            mine = pl.ds(pl.multiple_of(start + i * 16, 16), 16)
            theirs = pl.ds(pl.multiple_of(at + i * 16, 16), 16)
            buf[mine, :] = (buf[mine, :].astype(F32) + other[theirs, :].astype(F32)).astype(BF16)
            return carry

        lax.fori_loop(0, size // 16, per_rows, 0)

    def scatter_start(half):
        through = [
            remote(part.at[row_slot(half, 3, 0, 32)], ptl.at[pl.ds(half * 32, 32)], r_right),
            remote(part.at[row_slot(half, 3, 32, 32)], ptr.at[pl.ds(half * 32, 32)], r_left),
        ]
        plain = [
            remote(part.at[row_slot(half, 2, 32, 32)], pfl.at[pl.ds(half * 64 + 32, 32)], r_right),
            remote(part.at[row_slot(half, 1, 0, 32)], pfr.at[pl.ds(half * 64, 32)], r_left),
        ]
        return through, plain

    def scatter_add(half, through):
        through[0].wait_recv()
        add_into(part, half * 256 + 2 * HALF, ptl, half * 32, 32)
        a = remote(part.at[row_slot(half, 2, 0, 32)], pfl.at[pl.ds(half * 64, 32)], r_right)
        through[1].wait_recv()
        add_into(part, half * 256 + HALF + 32, ptr, half * 32, 32)
        b = remote(part.at[row_slot(half, 1, 32, 32)], pfr.at[pl.ds(half * 64 + 32, 32)], r_left)
        return a, b

    def scatter_end(half, copies):
        for copy in copies:
            copy.wait_recv()

        def per_rows(i, carry):
            mine = pl.ds(pl.multiple_of(half * 256 + i * 16, 16), 16)
            got = pl.ds(pl.multiple_of(half * 64 + i * 16, 16), 16)
            ret_send[got, :] = (
                part[mine, :].astype(F32) + pfl[got, :].astype(F32) + pfr[got, :].astype(F32)
            ).astype(BF16)
            return carry

        lax.fori_loop(0, HALF // 16, per_rows, 0)
        back = []
        for k in range(half * 4, half * 4 + 4):
            piece_rows = pl.ds(k * CAP, CAP)
            if k == 0:
                ret[piece_rows, :] = ret_send[piece_rows, :]
            else:
                source = (lax.rem(dp + k, 8), ex)
                back.append(remote(ret_send.at[piece_rows], ret.at[piece_rows], source))
        return back

    def weight_grads(s):
        two = pl.ds(s * 192, 192)
        one = pl.ds(s * HID, HID)

        def per_cols(i, carry):
            cols = pl.ds(pl.multiple_of(i * COLS, COLS), COLS)
            pg[two, cols] = dot(act[two, :], rn[:, cols], 1, 0).astype(BF16)
            pd[one, cols] = dot(hid[one, :], rg[:, cols], 1, 0).astype(BF16)
            return carry

        lax.fori_loop(0, D // COLS, per_cols, 0)

    for copy in last_a:
        copy.wait_recv()
    activations(0)
    partials(0)
    through_a, plain_a = scatter_start(0)

    for copy in last_b:
        copy.wait_recv()
    activations(1)
    summed_a = scatter_add(0, through_a)
    partials(1)
    through_b, plain_b = scatter_start(1)
    back = scatter_end(0, [*plain_a, *summed_a])

    weight_grads(3)
    grad_through = [
        remote(pg.at[pl.ds(3 * 192, HID)], gtl.at[pl.ds(0, HID)], w_right),
        remote(pg.at[pl.ds(3 * 192 + HID, HID)], gtr.at[pl.ds(0, HID)], w_left),
        remote(pd.at[pl.ds(3 * HID, 48)], gtl.at[pl.ds(HID, 48)], w_right),
        remote(pd.at[pl.ds(3 * HID + 48, 48)], gtr.at[pl.ds(HID, 48)], w_left),
    ]
    summed_b = scatter_add(1, through_b)
    weight_grads(2)
    grad_plain = [
        remote(pg.at[pl.ds(2 * 192 + HID, HID)], gfl.at[pl.ds(HID, HID)], w_right),
        remote(pd.at[pl.ds(2 * HID + 48, 48)], gfl.at[pl.ds(2 * HID + 48, 48)], w_right),
    ]
    weight_grads(1)
    grad_plain += [
        remote(pg.at[pl.ds(192, HID)], gfr.at[pl.ds(0, HID)], w_left),
        remote(pd.at[pl.ds(HID, 48)], gfr.at[pl.ds(2 * HID, 48)], w_left),
    ]
    back += scatter_end(1, [*plain_b, *summed_b])
    weight_grads(0)

    grad_through[0].wait_recv()
    add_into(pg, 2 * 192, gtl, 0, HID)
    grad_summed = [remote(pg.at[pl.ds(2 * 192, HID)], gfl.at[pl.ds(0, HID)], w_right)]
    grad_through[1].wait_recv()
    add_into(pg, 192 + HID, gtr, 0, HID)
    grad_summed.append(remote(pg.at[pl.ds(192 + HID, HID)], gfr.at[pl.ds(HID, HID)], w_left))
    grad_through[2].wait_recv()
    add_into(pd, 2 * HID, gtl, HID, 48)
    grad_summed.append(remote(pd.at[pl.ds(2 * HID, 48)], gfl.at[pl.ds(2 * HID, 48)], w_right))
    grad_through[3].wait_recv()
    add_into(pd, HID + 48, gtr, HID, 48)
    grad_summed.append(remote(pd.at[pl.ds(HID + 48, 48)], gfr.at[pl.ds(2 * HID + 48, 48)], w_left))

    for copy in back:
        copy.wait_recv()
    scale = inv[:, 0:1]

    def scaled(i, total):
        cols = pl.ds(pl.multiple_of(i * COLS, COLS), COLS)
        q = dot(place[...], ret[:, cols], 1, 0) * gain_ref[:, cols]
        qbuf[:, cols] = q
        return total + jnp.sum(q * (tok[:, cols].astype(F32) * scale), axis=-1, keepdims=True)

    total = lax.fori_loop(0, D // COLS, scaled, jnp.zeros((TOK, 1), F32))
    mean = total * (1.0 / D)

    def moved(i, carry):
        cols = pl.ds(pl.multiple_of(i * COLS, COLS), COLS)
        unit = tok[:, cols].astype(F32) * scale
        out_t[:, cols] = (cot[:, cols].astype(F32) + scale * (qbuf[:, cols] - unit * mean)).astype(BF16)
        return carry

    lax.fori_loop(0, D // COLS, moved, 0)
    outs = [local(out_t, gt_hbm)]

    def grad_end(buf, at, got, copies, dst):
        for copy in copies:
            copy.wait_recv()
        add_three(buf, at, got)
        outs.append(local(buf.at[pl.ds(at, HID)], dst))

    def add_three(buf, at, got):
        def per_rows(i, carry):
            mine = pl.ds(pl.multiple_of(at + i * 16, 16), 16)
            theirs = pl.ds(pl.multiple_of(got + i * 16, 16), 16)
            buf[mine, :] = (
                buf[mine, :].astype(F32) + gfl[theirs, :].astype(F32) + gfr[theirs, :].astype(F32)
            ).astype(BF16)
            return carry

        lax.fori_loop(0, HID // 16, per_rows, 0)

    grad_end(pg, 0, 0, [grad_summed[0], grad_plain[2]], gg_hbm)
    grad_end(pg, HID, HID, [grad_plain[0], grad_summed[1]], gu_hbm)
    grad_end(pd, 0, 2 * HID, [grad_plain[1], grad_plain[3], grad_summed[2], grad_summed[3]], gd_hbm)

    for copy in outs:
        copy.wait()
    for copy in sent:
        copy.wait_send()


def on_device(
    tokens, norm_gain, routes, route_weight, gate_weight, up_weight, down_weight, cotangent
):
    any_spec = pl.BlockSpec(memory_space=pl.ANY)
    vmem_spec = pl.BlockSpec(memory_space=pltpu.VMEM)
    rows = lambda n, t=BF16: pltpu.VMEM((n, D), t)
    outs = pl.pallas_call(
        kernel,
        out_shape=(
            jax.ShapeDtypeStruct((TOK, D), BF16),
            jax.ShapeDtypeStruct((HID, D), BF16),
            jax.ShapeDtypeStruct((HID, D), BF16),
            jax.ShapeDtypeStruct((HID, D), BF16),
        ),
        in_specs=[any_spec, any_spec, vmem_spec, vmem_spec, vmem_spec, any_spec, any_spec, any_spec],
        out_specs=(any_spec,) * 4,
        scratch_shapes=[
            rows(TOK), rows(TOK), rows(TOK), rows(TOK), rows(TOK), rows(TOK),
            pltpu.VMEM((TOK, TOK), BF16), pltpu.VMEM((TOK, 128), F32),
            rows(512), rows(512), rows(768), rows(384),
            pltpu.VMEM((192, 256), F32), pltpu.VMEM((8, 128), F32),
            pltpu.VMEM((768, 512), BF16), pltpu.VMEM((256, 768), BF16), pltpu.VMEM((384, 512), BF16),
            rows(512), rows(64), rows(64), rows(128), rows(128),
            rows(TOK), rows(TOK), rows(TOK, F32), rows(TOK),
            rows(768), rows(384), rows(144), rows(144), rows(288), rows(288),
            pltpu.SemaphoreType.DMA((N_REMOTE,)),
            pltpu.SemaphoreType.DMA((N_REMOTE,)),
            pltpu.SemaphoreType.DMA((N_LOCAL,)),
        ],
        compiler_params=pltpu.CompilerParams(
            collective_id=0, has_side_effects=True, vmem_limit_bytes=63 * 2**20
        ),
        cost_estimate=pl.CostEstimate(flops=13 * 10**9, bytes_accessed=9 * 2**20, transcendentals=2**18),
        name="learner_step",
    )(
        tokens, cotangent, norm_gain.reshape(1, D), routes, route_weight,
        gate_weight[0], up_weight[0], down_weight[0],
    )
    return (outs[0], outs[1][None], outs[2][None], outs[3][None])


def solution(mesh):
    token_spec = P(("dp", "expert"), None)
    weight_spec = P("dp", "expert", None)
    return jax.shard_map(
        on_device,
        mesh=mesh,
        in_specs=(token_spec, P(), token_spec, token_spec, weight_spec, weight_spec, weight_spec, token_spec),
        out_specs=(token_spec, weight_spec, weight_spec, weight_spec),
        check_vma=False,
    )
```

```python
import functools

import jax
import jax.numpy as jnp
from jax import lax
from jax.experimental import pallas as pl
from jax.experimental.pallas import tpu as pltpu
from jax.sharding import PartitionSpec as P

MESH = pl.DeviceIdType.MESH
F32, BF16 = jnp.float32, jnp.bfloat16
D = 4096
TOK = 128
CAP = 16
HID = 96
HALF = 64
COLS = 512
SLOTS = 4

N_REMOTE = 80
N_LOCAL = 16


def dot(left, right, left_dim, right_dim):
    return lax.dot_general(
        left, right, (((left_dim,), (right_dim,)), ((), ())), preferred_element_type=F32
    )


def kernel(
    tok_hbm, cot_hbm, gain_hbm, routes_hbm, rw_hbm, gate_hbm, up_hbm, down_hbm,
    gt_out, gg_out, gu_out, gd_out,
    gain_ref, routes_ref, rw_ref, tok, cot, norm, rgrad, send_n, send_g, place, place_t, weight, inv,
    rn, rg, wgu, wd, pre, hg, act, act_t, hid,
    part, ptl, ptr, pfl, pfr, ret_send, ret, qbuf,
    pg, pd, gtl, gtr, gfl, gfr,
    ssem, rsem, lsem,
):
    dp = lax.axis_index("dp")
    ex = lax.axis_index("expert")
    core = lax.rem(dp, 2)
    rstride = 1 + 3 * core
    wstride = 4 - 3 * core
    rpos = lax.rem(lax.div(ex, rstride), 4)
    wpos = lax.rem(lax.div(ex, wstride), 4)
    r_right = (dp, ex + rstride * (lax.rem(rpos + 1, 4) - rpos))
    r_left = (dp, ex + rstride * (lax.rem(rpos + 3, 4) - rpos))
    w_right = (dp, ex + wstride * (lax.rem(wpos + 1, 4) - wpos))
    w_left = (dp, ex + wstride * (lax.rem(wpos + 3, 4) - wpos))

    count = [0, 0]
    sent = []

    def local(src, dst):
        copy = pltpu.make_async_copy(src, dst, lsem.at[count[1]])
        count[1] += 1
        copy.start()
        return copy

    def remote(src, dst, device):
        copy = pltpu.make_async_remote_copy(
            src_ref=src, dst_ref=dst, send_sem=ssem.at[count[0]], recv_sem=rsem.at[count[0]],
            device_id=device, device_id_type=MESH,
        )
        count[0] += 1
        copy.start()
        sent.append(copy)
        return copy

    barrier = pltpu.get_barrier_semaphore()
    partners = [r_right, r_left, w_right, w_left]
    partners += [(lax.rem(dp + k, 8), ex) for k in range(1, 8)]
    for device in partners:
        pl.semaphore_signal(barrier, inc=1, device_id=device, device_id_type=MESH)
    small_in = [local(routes_hbm, routes_ref), local(rw_hbm, rw_ref), local(gain_hbm, gain_ref)]
    tok_in = local(tok_hbm, tok)
    cot_in = local(cot_hbm, cot)
    pl.semaphore_wait(barrier, len(partners))

    w_from_left, w_from_right = [], []
    places = [(gate_hbm, wgu, 192, 0), (up_hbm, wgu, 192, 96), (down_hbm, wd, 96, 0)]
    for src, buf, step, at in places:
        w_from_left.append(remote(src, buf.at[pl.ds(step + at, HID)], w_right))
        w_from_right.append(remote(src, buf.at[pl.ds(2 * step + at, HID)], w_left))
    w_own = [local(src, buf.at[pl.ds(at, HID)]) for src, buf, step, at in places]

    for copy in small_in:
        copy.wait()
    chosen = routes_ref[...]
    lane = lax.broadcasted_iota(jnp.int32, (TOK, TOK), 1)
    sub = lax.broadcasted_iota(jnp.int32, (TOK, TOK), 0)
    onehot = (chosen == sub).astype(F32)
    earlier = dot(onehot.astype(BF16), (sub < lane).astype(F32).astype(BF16), 1, 0)
    position = jnp.sum(earlier * onehot, axis=0, keepdims=True)
    piece = jnp.bitwise_and(dp - chosen + 8, 7)
    slot = piece.astype(F32) * CAP + position
    placing = (slot == sub.astype(F32)).astype(F32)
    place[...] = placing.T.astype(BF16)
    place_t[...] = placing.astype(BF16)
    weight[...] = jnp.broadcast_to(rw_ref[...], (TOK, TOK)).T

    tok_in.wait()
    cot_in.wait()

    def norm_rows(i, carry):
        rows = pl.ds(pl.multiple_of(i * 16, 16), 16)
        x = tok[rows, :].astype(F32)
        scale = lax.rsqrt(jnp.mean(x * x, axis=-1, keepdims=True) + 1e-06)
        inv[rows, :] = jnp.broadcast_to(scale, (16, 128))
        norm[rows, :] = ((x * scale) * gain_ref[...]).astype(BF16)
        rgrad[rows, :] = (weight[rows, 0:1] * cot[rows, :].astype(F32)).astype(BF16)
        return carry

    lax.fori_loop(0, TOK // 16, norm_rows, 0)

    placing_t = place_t[...]

    def place_rows(i, carry):
        cols = pl.ds(pl.multiple_of(i * COLS, COLS), COLS)
        send_n[:, cols] = dot(placing_t, norm[:, cols], 1, 0).astype(BF16)
        send_g[:, cols] = dot(placing_t, rgrad[:, cols], 1, 0).astype(BF16)
        return carry

    lax.fori_loop(0, D // COLS, place_rows, 0)

    def at_piece(k):
        return pl.ds((k // 4) * 256 + (k % 4) * CAP, CAP)

    arrive = {0: [], 1: []}
    rn[at_piece(0), :] = send_n[pl.ds(0, CAP), :]
    rg[at_piece(0), :] = send_g[pl.ds(0, CAP), :]
    for k in range(1, 8):
        owner = (lax.rem(dp + 8 - k, 8), ex)
        piece_rows = pl.ds(k * CAP, CAP)
        arrive[k // 4].append(remote(send_n.at[piece_rows], rn.at[at_piece(k)], owner))
        arrive[k // 4].append(remote(send_g.at[piece_rows], rg.at[at_piece(k)], owner))

    def row_slot(half, s, at=0, size=HALF):
        return pl.ds(half * 256 + s * HALF + at, size)

    def send_own(buf, half):
        return (
            remote(buf.at[row_slot(half, 0)], buf.at[row_slot(half, 1)], r_right),
            remote(buf.at[row_slot(half, 0)], buf.at[row_slot(half, 2)], r_left),
        )

    def pass_on(buf, half, first):
        first[0].wait_recv()
        a = remote(buf.at[row_slot(half, 1, 0, 32)], buf.at[row_slot(half, 3, 0, 32)], r_right)
        first[1].wait_recv()
        b = remote(buf.at[row_slot(half, 2, 32, 32)], buf.at[row_slot(half, 3, 32, 32)], r_left)
        return a, b

    w_from_left[0].wait_recv()
    w_last = [remote(wgu.at[pl.ds(192, HID)], wgu.at[pl.ds(3 * 192, HID)], w_right)]
    w_from_right[0].wait_recv()
    w_from_left[1].wait_recv()
    w_from_right[1].wait_recv()
    w_last.append(remote(wgu.at[pl.ds(2 * 192 + 96, HID)], wgu.at[pl.ds(3 * 192 + 96, HID)], w_left))
    for copy in arrive[0]:
        copy.wait_recv()
    own_an = send_own(rn, 0)
    own_ag = send_own(rg, 0)
    w_from_left[2].wait_recv()
    w_last.append(remote(wd.at[pl.ds(HID, 48)], wd.at[pl.ds(3 * HID, 48)], w_right))
    w_from_right[2].wait_recv()
    w_last.append(remote(wd.at[pl.ds(2 * HID + 48, 48)], wd.at[pl.ds(3 * HID + 48, 48)], w_left))
    for copy in arrive[1]:
        copy.wait_recv()
    own_bn = send_own(rn, 1)
    last_a = [*pass_on(rn, 0, own_an), *pass_on(rg, 0, own_ag)]
    own_bg = send_own(rg, 1)
    last_b = [*pass_on(rn, 1, own_bn)]

    for copy in w_own:
        copy.wait()
    for copy in w_last:
        copy.wait_recv()

    def products(half):
        rows = pl.ds(half * 256, 256)
        pre[...] = dot(wgu[...], rn[rows, :], 1, 1)
        hg[...] = dot(wd[...], rg[rows, :], 1, 1)

    def activations(half):
        rows = pl.ds(half * 256, 256)

        def per_slot(s, carry):
            one = pl.ds(pl.multiple_of(s * HID, HID), HID)
            gate_rows = pl.ds(pl.multiple_of(s * 192, 96), HID)
            up_rows = pl.ds(pl.multiple_of(s * 192 + HID, 96), HID)
            gate, up, hidden_grad = pre[gate_rows, :], pre[up_rows, :], hg[one, :]
            sig = jax.nn.sigmoid(gate)
            active = gate * sig
            hid[one, rows] = (active * up).astype(BF16)
            act[gate_rows, rows] = (hidden_grad * up * sig * (1.0 + gate * (1.0 - sig))).astype(BF16)
            act[up_rows, rows] = (hidden_grad * active).astype(BF16)
            return carry

        lax.fori_loop(0, SLOTS, per_slot, 0)

    def partials(half):
        rows = pl.ds(half * 256, 256)
        act_t[...] = act[:, rows].T

        def per_cols(i, carry):
            cols = pl.ds(pl.multiple_of(i * COLS, COLS), COLS)
            part[rows, cols] = dot(act_t[...], wgu[:, cols], 1, 0).astype(BF16)
            return carry

        lax.fori_loop(0, D // COLS, per_cols, 0)

    def add_into(buf, start, other, at, size):
        def per_rows(i, carry):
            mine = pl.ds(pl.multiple_of(start + i * 16, 16), 16)
            theirs = pl.ds(pl.multiple_of(at + i * 16, 16), 16)
            buf[mine, :] = (buf[mine, :].astype(F32) + other[theirs, :].astype(F32)).astype(BF16)
            return carry

        lax.fori_loop(0, size // 16, per_rows, 0)

    def scatter_start(half):
        through = [
            remote(part.at[row_slot(half, 3, 0, 32)], ptl.at[pl.ds(half * 32, 32)], r_right),
            remote(part.at[row_slot(half, 3, 32, 32)], ptr.at[pl.ds(half * 32, 32)], r_left),
        ]
        plain = [
            remote(part.at[row_slot(half, 2, 32, 32)], pfl.at[pl.ds(half * 64 + 32, 32)], r_right),
            remote(part.at[row_slot(half, 1, 0, 32)], pfr.at[pl.ds(half * 64, 32)], r_left),
        ]
        return through, plain

    def scatter_add(half, through):
        through[0].wait_recv()
        add_into(part, half * 256 + 2 * HALF, ptl, half * 32, 32)
        a = remote(part.at[row_slot(half, 2, 0, 32)], pfl.at[pl.ds(half * 64, 32)], r_right)
        through[1].wait_recv()
        add_into(part, half * 256 + HALF + 32, ptr, half * 32, 32)
        b = remote(part.at[row_slot(half, 1, 32, 32)], pfr.at[pl.ds(half * 64 + 32, 32)], r_left)
        return a, b

    def scatter_end(half, copies):
        for copy in copies:
            copy.wait_recv()

        def per_rows(i, carry):
            mine = pl.ds(pl.multiple_of(half * 256 + i * 16, 16), 16)
            got = pl.ds(pl.multiple_of(half * 64 + i * 16, 16), 16)
            ret_send[got, :] = (
                part[mine, :].astype(F32) + pfl[got, :].astype(F32) + pfr[got, :].astype(F32)
            ).astype(BF16)
            return carry

        lax.fori_loop(0, HALF // 16, per_rows, 0)
        back = []
        for k in range(half * 4, half * 4 + 4):
            piece_rows = pl.ds(k * CAP, CAP)
            if k == 0:
                ret[piece_rows, :] = ret_send[piece_rows, :]
            else:
                source = (lax.rem(dp + k, 8), ex)
                back.append(remote(ret_send.at[piece_rows], ret.at[piece_rows], source))
        return back

    def weight_grads(s):
        two = pl.ds(s * 192, 192)
        one = pl.ds(s * HID, HID)

        def per_cols(i, carry):
            cols = pl.ds(pl.multiple_of(i * COLS, COLS), COLS)
            pg[two, cols] = dot(act[two, :], rn[:, cols], 1, 0).astype(BF16)
            pd[one, cols] = dot(hid[one, :], rg[:, cols], 1, 0).astype(BF16)
            return carry

        lax.fori_loop(0, D // COLS, per_cols, 0)

    for copy in last_a:
        copy.wait_recv()
    products(0)
    activations(0)
    last_b += [*pass_on(rg, 1, own_bg)]
    partials(0)
    through_a, plain_a = scatter_start(0)

    for copy in last_b:
        copy.wait_recv()
    products(1)
    summed_a = scatter_add(0, through_a)
    activations(1)
    partials(1)
    through_b, plain_b = scatter_start(1)
    weight_grads(3)
    grad_through = [
        remote(pg.at[pl.ds(3 * 192, HID)], gtl.at[pl.ds(0, HID)], w_right),
        remote(pg.at[pl.ds(3 * 192 + HID, HID)], gtr.at[pl.ds(0, HID)], w_left),
        remote(pd.at[pl.ds(3 * HID, 48)], gtl.at[pl.ds(HID, 48)], w_right),
        remote(pd.at[pl.ds(3 * HID + 48, 48)], gtr.at[pl.ds(HID, 48)], w_left),
    ]
    back = scatter_end(0, [*plain_a, *summed_a])
    summed_b = scatter_add(1, through_b)
    weight_grads(2)
    grad_plain = [
        remote(pg.at[pl.ds(2 * 192 + HID, HID)], gfl.at[pl.ds(HID, HID)], w_right),
        remote(pd.at[pl.ds(2 * HID + 48, 48)], gfl.at[pl.ds(2 * HID + 48, 48)], w_right),
    ]
    weight_grads(1)
    grad_plain += [
        remote(pg.at[pl.ds(192, HID)], gfr.at[pl.ds(0, HID)], w_left),
        remote(pd.at[pl.ds(HID, 48)], gfr.at[pl.ds(2 * HID, 48)], w_left),
    ]
    back += scatter_end(1, [*plain_b, *summed_b])
    weight_grads(0)

    grad_through[0].wait_recv()
    add_into(pg, 2 * 192, gtl, 0, HID)
    grad_summed = [remote(pg.at[pl.ds(2 * 192, HID)], gfl.at[pl.ds(0, HID)], w_right)]
    grad_through[1].wait_recv()
    add_into(pg, 192 + HID, gtr, 0, HID)
    grad_summed.append(remote(pg.at[pl.ds(192 + HID, HID)], gfr.at[pl.ds(HID, HID)], w_left))
    grad_through[2].wait_recv()
    add_into(pd, 2 * HID, gtl, HID, 48)
    grad_summed.append(remote(pd.at[pl.ds(2 * HID, 48)], gfl.at[pl.ds(2 * HID, 48)], w_right))
    grad_through[3].wait_recv()
    add_into(pd, HID + 48, gtr, HID, 48)
    grad_summed.append(remote(pd.at[pl.ds(HID + 48, 48)], gfr.at[pl.ds(2 * HID + 48, 48)], w_left))

    for copy in back:
        copy.wait_recv()
    scale = inv[:, 0:1]

    def scaled(i, total):
        cols = pl.ds(pl.multiple_of(i * COLS, COLS), COLS)
        q = dot(place[...], ret[:, cols], 1, 0) * gain_ref[:, cols]
        qbuf[:, cols] = q
        return total + jnp.sum(q * (tok[:, cols].astype(F32) * scale), axis=-1, keepdims=True)

    total = lax.fori_loop(0, D // COLS, scaled, jnp.zeros((TOK, 1), F32))
    mean = total * (1.0 / D)

    def moved(i, carry):
        cols = pl.ds(pl.multiple_of(i * COLS, COLS), COLS)
        unit = tok[:, cols].astype(F32) * scale
        gt_out[:, cols] = (cot[:, cols].astype(F32) + scale * (qbuf[:, cols] - unit * mean)).astype(BF16)
        return carry

    lax.fori_loop(0, D // COLS, moved, 0)

    def grad_end(out, buf, first, got, size, copies):
        for copy in copies:
            copy.wait_recv()

        def per_rows(i, carry):
            mine = pl.ds(pl.multiple_of(first + i * 16, 16), 16)
            theirs = pl.ds(pl.multiple_of(got + first + i * 16, 16), 16)
            own = pl.ds(pl.multiple_of(got % 192 + first + i * 16, 16), 16)
            out[mine, :] = (
                buf[own, :].astype(F32) + gfl[theirs, :].astype(F32) + gfr[theirs, :].astype(F32)
            ).astype(BF16)
            return carry

        lax.fori_loop(0, size // 16, per_rows, 0)

    for copy in sent[: -len(grad_summed)]:
        copy.wait_send()

    grad_end(gg_out, pg, 0, 0, HID, [grad_summed[0], grad_plain[2]])
    grad_end(gu_out, pg, 0, HID, HID, [grad_plain[0], grad_summed[1]])
    grad_end(gd_out, pd, 0, 2 * HID, 48, [grad_plain[3], grad_summed[2]])
    grad_end(gd_out, pd, 48, 2 * HID, 48, [grad_plain[1], grad_summed[3]])

    for copy in grad_summed:
        copy.wait_send()


def hand_over(*refs):
    copies = []
    for i in range(4):
        rows = refs[i].shape[0] // 2
        for j in range(2):
            part = pl.ds(j * rows, rows)
            copies.append(pltpu.make_async_copy(refs[i].at[part], refs[4 + i].at[part], refs[8].at[2 * i + j]))
    for copy in copies:
        copy.start()
    for copy in copies:
        copy.wait()


def on_device(
    tokens, norm_gain, routes, route_weight, gate_weight, up_weight, down_weight, cotangent
):
    any_spec = pl.BlockSpec(memory_space=pl.ANY)
    vmem_spec = pl.BlockSpec(memory_space=pltpu.VMEM)
    rows = lambda n, t=BF16: pltpu.VMEM((n, D), t)
    outs = pl.pallas_call(
        kernel,
        out_shape=(
            pltpu.VMEM((TOK, D), BF16),
            pltpu.VMEM((HID, D), BF16),
            pltpu.VMEM((HID, D), BF16),
            pltpu.VMEM((HID, D), BF16),
        ),
        in_specs=[any_spec] * 8,
        out_specs=(vmem_spec,) * 4,
        scratch_shapes=[
            pltpu.VMEM((1, D), F32), pltpu.VMEM((1, TOK), jnp.int32), pltpu.VMEM((1, TOK), F32),
            rows(TOK), rows(TOK), rows(TOK), rows(TOK), rows(TOK), rows(TOK),
            pltpu.VMEM((TOK, TOK), BF16), pltpu.VMEM((TOK, TOK), BF16),
            pltpu.VMEM((TOK, TOK), F32), pltpu.VMEM((TOK, 128), F32),
            rows(512), rows(512), rows(768), rows(384),
            pltpu.VMEM((768, 256), F32), pltpu.VMEM((384, 256), F32),
            pltpu.VMEM((768, 512), BF16), pltpu.VMEM((256, 768), BF16), pltpu.VMEM((384, 512), BF16),
            rows(512), rows(64), rows(64), rows(128), rows(128),
            rows(TOK), rows(TOK), rows(TOK, F32),
            rows(768), rows(384), rows(144), rows(144), rows(288), rows(288),
            pltpu.SemaphoreType.DMA((N_REMOTE,)),
            pltpu.SemaphoreType.DMA((N_REMOTE,)),
            pltpu.SemaphoreType.DMA((N_LOCAL,)),
        ],
        compiler_params=pltpu.CompilerParams(
            collective_id=0, has_side_effects=True, vmem_limit_bytes=56 * 2**20
        ),
        cost_estimate=pl.CostEstimate(flops=13 * 10**9, bytes_accessed=9 * 2**20, transcendentals=2**18),
        name="learner_step",
    )(
        tokens, cotangent, norm_gain.reshape(1, D), routes.reshape(1, TOK), route_weight.reshape(1, TOK),
        gate_weight[0], up_weight[0], down_weight[0],
    )
    outs = pl.pallas_call(
        hand_over,
        out_shape=tuple(jax.ShapeDtypeStruct(out.shape, out.dtype) for out in outs),
        in_specs=[vmem_spec] * 4,
        out_specs=(any_spec,) * 4,
        scratch_shapes=[pltpu.SemaphoreType.DMA((8,))],
        name="hand_over",
    )(*(pltpu.with_memory_space_constraint(out, pltpu.VMEM) for out in outs))
    return (outs[0], outs[1][None], outs[2][None], outs[3][None])


def solution(mesh):
    token_spec = P(("dp", "expert"), None)
    weight_spec = P("dp", "expert", None)
    return jax.shard_map(
        on_device,
        mesh=mesh,
        in_specs=(token_spec, P(), token_spec, token_spec, weight_spec, weight_spec, weight_spec, token_spec),
        out_specs=(token_spec, weight_spec, weight_spec, weight_spec),
        check_vma=False,
    )
```

```python
import functools

import jax
import jax.numpy as jnp
from jax import lax
from jax.experimental import pallas as pl
from jax.experimental.pallas import tpu as pltpu
from jax.sharding import PartitionSpec as P

MESH = pl.DeviceIdType.MESH
F32, BF16 = jnp.float32, jnp.bfloat16
D = 4096
TOK = 128
CAP = 16
HID = 96
HALF = 64
COLS = 512
SLOTS = 4

N_SEND, N_RECV, N_LOCAL = 8, 34, 8


def dot(left, right, left_dim, right_dim):
    return lax.dot_general(
        left, right, (((left_dim,), (right_dim,)), ((), ())), preferred_element_type=F32
    )


def kernel(
    tok_hbm, cot_hbm, gain_hbm, routes_hbm, rw_hbm, gate_hbm, up_hbm, down_hbm,
    gt_out, gg_out, gu_out, gd_out,
    gain_ref, routes_ref, rw_ref, tok, cot, norm, rgrad, send, place, place_t, weight, inv,
    x, w, pre, hg, act, act_t, hid,
    part, ptl, ptr, pfl, pfr, ret_send, ret, qbuf,
    g, gtl, gtr, gfl, gfr,
    ssem, rsem, lsem,
):
    dp = lax.axis_index("dp")
    ex = lax.axis_index("expert")
    core = lax.rem(dp, 2)
    rstride = 1 + 3 * core
    wstride = 4 - 3 * core
    rpos = lax.rem(lax.div(ex, rstride), 4)
    wpos = lax.rem(lax.div(ex, wstride), 4)
    r_right = (dp, ex + rstride * (lax.rem(rpos + 1, 4) - rpos))
    r_left = (dp, ex + rstride * (lax.rem(rpos + 3, 4) - rpos))
    w_right = (dp, ex + wstride * (lax.rem(wpos + 1, 4) - wpos))
    w_left = (dp, ex + wstride * (lax.rem(wpos + 3, 4) - wpos))

    count = [0, 0]

    def local(src, dst):
        copy = pltpu.make_async_copy(src, dst, lsem.at[count[1]])
        count[1] += 1
        copy.start()
        return copy

    def new():
        count[0] += 1
        return count[0] - 1

    def describe(src, dst, device, sender, receiver):
        return pltpu.make_async_remote_copy(
            src_ref=src, dst_ref=dst, send_sem=ssem.at[sender], recv_sem=rsem.at[receiver],
            device_id=device, device_id_type=MESH,
        )

    def remote(src, dst, device, sender, receiver=None):
        copy = describe(src, dst, device, sender, new() if receiver is None else receiver)
        copy.start()
        return copy

    def arrived(ref, receiver):
        describe(ref, ref, r_right, 0, receiver).wait_recv()

    def left_here(ref, sender):
        describe(ref, ref, r_right, sender, 0).wait_send()

    barrier = pltpu.get_barrier_semaphore()
    partners = [r_right, r_left, w_right, w_left]
    partners += [(lax.rem(dp + k, 8), ex) for k in range(1, 8)]
    for device in partners:
        pl.semaphore_signal(barrier, inc=1, device_id=device, device_id_type=MESH)
    small_in = [local(routes_hbm, routes_ref), local(rw_hbm, rw_ref), local(gain_hbm, gain_ref)]
    tok_in = local(tok_hbm, tok)
    cot_in = local(cot_hbm, cot)
    pl.semaphore_wait(barrier, len(partners))

    gate_r = remote(gate_hbm, w.at[1, pl.ds(0, HID)], w_right, 0)
    down_l = remote(down_hbm, w.at[2, pl.ds(2 * HID, HID)], w_left, 0)
    up_r = remote(up_hbm, w.at[1, pl.ds(HID, HID)], w_right, 0)
    up_l = remote(up_hbm, w.at[2, pl.ds(HID, HID)], w_left, 0)
    down_r = remote(down_hbm, w.at[1, pl.ds(2 * HID, HID)], w_right, 0)
    gate_l = remote(gate_hbm, w.at[2, pl.ds(0, HID)], w_left, 0)
    w_own = [local(src, w.at[0, pl.ds(i * HID, HID)]) for i, src in enumerate((gate_hbm, up_hbm, down_hbm))]

    for copy in small_in:
        copy.wait()
    chosen = routes_ref[...]
    lane = lax.broadcasted_iota(jnp.int32, (TOK, TOK), 1)
    sub = lax.broadcasted_iota(jnp.int32, (TOK, TOK), 0)
    onehot = (chosen == sub).astype(F32)
    earlier = dot(onehot.astype(BF16), (sub < lane).astype(F32).astype(BF16), 1, 0)
    position = jnp.sum(earlier * onehot, axis=0, keepdims=True)
    piece = jnp.bitwise_and(dp - chosen + 8, 7)
    slot = piece.astype(F32) * CAP + position
    placing = (slot == sub.astype(F32)).astype(F32)
    place[...] = placing.T.astype(BF16)
    place_t[...] = placing.astype(BF16)
    weight[...] = jnp.broadcast_to(rw_ref[...], (TOK, TOK)).T

    tok_in.wait()
    cot_in.wait()

    def norm_rows(i, carry):
        rows = pl.ds(pl.multiple_of(i * 16, 16), 16)
        x = tok[rows, :].astype(F32)
        scale = lax.rsqrt(jnp.mean(x * x, axis=-1, keepdims=True) + 1e-06)
        inv[rows, :] = jnp.broadcast_to(scale, (16, 128))
        norm[rows, :] = ((x * scale) * gain_ref[...]).astype(BF16)
        rgrad[rows, :] = (weight[rows, 0:1] * cot[rows, :].astype(F32)).astype(BF16)
        return carry

    lax.fori_loop(0, TOK // 16, norm_rows, 0)

    placing_t = place_t[...]

    def place_rows(i, carry):
        cols = pl.ds(pl.multiple_of(i * COLS, COLS), COLS)
        send[:, 0, :, cols] = dot(placing_t, norm[:, cols], 1, 0).astype(BF16).reshape(8, CAP, COLS)
        send[:, 1, :, cols] = dot(placing_t, rgrad[:, cols], 1, 0).astype(BF16).reshape(8, CAP, COLS)
        return carry

    lax.fori_loop(0, D // COLS, place_rows, 0)

    x[0, 0, :, pl.ds(0, CAP), :] = send[0]
    pieces = [new(), new()]
    for k in range(1, 8):
        owner = (lax.rem(dp + 8 - k, 8), ex)
        remote(send.at[k], x.at[k // 4, 0, :, pl.ds((k % 4) * CAP, CAP)], owner, 1, pieces[k // 4])

    w_far = new()
    gate_r.wait_recv()
    down_l.wait_recv()
    up_r.wait_recv()
    remote(w.at[1, pl.ds(0, 144)], w.at[3, pl.ds(0, 144)], w_right, 2, w_far)
    up_l.wait_recv()
    remote(w.at[2, pl.ds(144, 144)], w.at[3, pl.ds(144, 144)], w_left, 2, w_far)

    arrived(x.at[0, 0, :, pl.ds(CAP, 3 * CAP)], pieces[0])
    a_r = remote(x.at[0, 0], x.at[0, 1], r_right, 3)
    a_l = remote(x.at[0, 0], x.at[0, 2], r_left, 3)
    arrived(x.at[1, 0], pieces[1])
    bn_r = remote(x.at[1, 0, 0], x.at[1, 1, 0], r_right, 3)
    bg_l = remote(x.at[1, 0, 1], x.at[1, 2, 1], r_left, 3)
    a_far, b_far = new(), new()
    a_r.wait_recv()
    remote(x.at[0, 1, 0], x.at[0, 3, 0], r_right, 4, a_far)
    bg_r = remote(x.at[1, 0, 1], x.at[1, 1, 1], r_right, 3)
    a_l.wait_recv()
    remote(x.at[0, 2, 1], x.at[0, 3, 1], r_left, 4, a_far)
    bn_l = remote(x.at[1, 0, 0], x.at[1, 2, 0], r_left, 3)
    bn_r.wait_recv()
    remote(x.at[1, 1, 0], x.at[1, 3, 0], r_right, 4, b_far)
    bg_l.wait_recv()
    remote(x.at[1, 2, 1], x.at[1, 3, 1], r_left, 4, b_far)

    def row_slot(half, s, at=0, size=HALF):
        return pl.ds(half * 256 + s * HALF + at, size)

    def products(half):
        pre[...] = dot(w[:, pl.ds(0, 192), :].reshape(768, D), x[half, :, 0].reshape(256, D), 1, 1)
        hg[...] = dot(w[:, pl.ds(192, HID), :].reshape(384, D), x[half, :, 1].reshape(256, D), 1, 1)

    def activations(half):
        rows = pl.ds(half * 256, 256)

        def per_slot(s, carry):
            one = pl.ds(pl.multiple_of(s * HID, HID), HID)
            gate_rows = pl.ds(pl.multiple_of(s * 192, 96), HID)
            up_rows = pl.ds(pl.multiple_of(s * 192 + HID, 96), HID)
            gate, up, hidden_grad = pre[gate_rows, :], pre[up_rows, :], hg[one, :]
            sig = jax.nn.sigmoid(gate)
            active = gate * sig
            hid[one, rows] = (active * up).astype(BF16)
            act[gate_rows, rows] = (hidden_grad * up * sig * (1.0 + gate * (1.0 - sig))).astype(BF16)
            act[up_rows, rows] = (hidden_grad * active).astype(BF16)
            return carry

        lax.fori_loop(0, SLOTS, per_slot, 0)

    def partials(half):
        rows = pl.ds(half * 256, 256)
        act_t[...] = act[:, rows].T

        def per_cols(i, carry):
            cols = pl.ds(pl.multiple_of(i * COLS, COLS), COLS)
            part[rows, cols] = dot(act_t[...], w[:, pl.ds(0, 192), cols].reshape(768, COLS), 1, 0).astype(BF16)
            return carry

        lax.fori_loop(0, D // COLS, per_cols, 0)

    def add_into(buf, start, other, at, size):
        def per_rows(i, carry):
            mine = pl.ds(pl.multiple_of(start + i * 16, 16), 16)
            theirs = pl.ds(pl.multiple_of(at + i * 16, 16), 16)
            buf[mine, :] = (buf[mine, :].astype(F32) + other[theirs, :].astype(F32)).astype(BF16)
            return carry

        lax.fori_loop(0, size // 16, per_rows, 0)

    def scatter_start(half):
        ends = [new(), new()]
        through = [
            remote(part.at[row_slot(half, 3, 0, 32)], ptl.at[pl.ds(half * 32, 32)], r_right, 5),
            remote(part.at[row_slot(half, 3, 32, 32)], ptr.at[pl.ds(half * 32, 32)], r_left, 5),
        ]
        remote(part.at[row_slot(half, 2, 32, 32)], pfl.at[pl.ds(half * 64 + 32, 32)], r_right, 5, ends[0])
        remote(part.at[row_slot(half, 1, 0, 32)], pfr.at[pl.ds(half * 64, 32)], r_left, 5, ends[1])
        return through, ends

    def scatter_add(half, through, ends):
        through[0].wait_recv()
        add_into(part, half * 256 + 2 * HALF, ptl, half * 32, 32)
        remote(part.at[row_slot(half, 2, 0, 32)], pfl.at[pl.ds(half * 64, 32)], r_right, 5, ends[0])
        through[1].wait_recv()
        add_into(part, half * 256 + HALF + 32, ptr, half * 32, 32)
        remote(part.at[row_slot(half, 1, 32, 32)], pfr.at[pl.ds(half * 64 + 32, 32)], r_left, 5, ends[1])

    back = new()

    def scatter_end(half, ends):
        arrived(pfl.at[pl.ds(half * 64, 64)], ends[0])
        arrived(pfr.at[pl.ds(half * 64, 64)], ends[1])

        def per_rows(i, carry):
            mine = pl.ds(pl.multiple_of(half * 256 + i * 16, 16), 16)
            got = pl.ds(pl.multiple_of(half * 64 + i * 16, 16), 16)
            ret_send[got, :] = (
                part[mine, :].astype(F32) + pfl[got, :].astype(F32) + pfr[got, :].astype(F32)
            ).astype(BF16)
            return carry

        lax.fori_loop(0, HALF // 16, per_rows, 0)
        for k in range(half * 4, half * 4 + 4):
            piece_rows = pl.ds(k * CAP, CAP)
            if k == 0:
                ret[piece_rows, :] = ret_send[piece_rows, :]
            else:
                remote(ret_send.at[piece_rows], ret.at[piece_rows], (lax.rem(dp + k, 8), ex), 6, back)

    def weight_grads(s):
        two = pl.ds(s * 192, 192)
        one = pl.ds(s * HID, HID)

        def per_cols(i, carry):
            cols = pl.ds(pl.multiple_of(i * COLS, COLS), COLS)
            g[s, pl.ds(0, 192), cols] = dot(act[two, :], x[:, :, 0, :, cols].reshape(512, COLS), 1, 0).astype(BF16)
            g[s, pl.ds(192, HID), cols] = dot(hid[one, :], x[:, :, 1, :, cols].reshape(512, COLS), 1, 0).astype(BF16)
            return carry

        lax.fori_loop(0, D // COLS, per_cols, 0)

    for copy in (*w_own,):
        copy.wait()
    down_r.wait_recv()
    gate_l.wait_recv()
    arrived(w.at[3], w_far)
    arrived(x.at[0, 3], a_far)
    products(0)
    activations(0)
    partials(0)
    through_a, ends_a = scatter_start(0)

    bg_r.wait_recv()
    bn_l.wait_recv()
    arrived(x.at[1, 3], b_far)
    products(1)
    scatter_add(0, through_a, ends_a)
    activations(1)
    partials(1)
    through_b, ends_b = scatter_start(1)
    weight_grads(3)
    top, low = pl.ds(0, 144), pl.ds(144, 144)
    grad_r = remote(g.at[3, top], gtl, w_right, 7)
    grad_l = remote(g.at[3, low], gtr, w_left, 7)
    scatter_end(0, ends_a)
    scatter_add(1, through_b, ends_b)
    weight_grads(2)
    plain_r = remote(g.at[2, low], gfl.at[low], w_right, 7)
    weight_grads(1)
    plain_l = remote(g.at[1, top], gfr.at[top], w_left, 7)
    scatter_end(1, ends_b)
    weight_grads(0)

    summed = []
    grad_r.wait_recv()
    for at, size in ((0, HID), (HID, 48)):
        add_into(g.at[2], at, gtl, at, size)
        rows = pl.ds(at, size)
        summed.append(remote(g.at[2, rows], gfl.at[rows], w_right, 7))
    grad_l.wait_recv()
    for at, size in ((0, HID), (HID, 48)):
        add_into(g.at[1], 144 + at, gtr, at, size)
        rows = pl.ds(144 + at, size)
        summed.append(remote(g.at[1, rows], gfr.at[rows], w_left, 7))

    arrived(ret.at[pl.ds(CAP, 7 * CAP)], back)
    scale = inv[:, 0:1]

    def scaled(i, total):
        cols = pl.ds(pl.multiple_of(i * COLS, COLS), COLS)
        q = dot(place[...], ret[:, cols], 1, 0) * gain_ref[:, cols]
        qbuf[:, cols] = q
        return total + jnp.sum(q * (tok[:, cols].astype(F32) * scale), axis=-1, keepdims=True)

    total = lax.fori_loop(0, D // COLS, scaled, jnp.zeros((TOK, 1), F32))
    mean = total * (1.0 / D)

    def moved(i, carry):
        cols = pl.ds(pl.multiple_of(i * COLS, COLS), COLS)
        unit = tok[:, cols].astype(F32) * scale
        gt_out[:, cols] = (cot[:, cols].astype(F32) + scale * (qbuf[:, cols] - unit * mean)).astype(BF16)
        return carry

    lax.fori_loop(0, D // COLS, moved, 0)

    def grad_end(out, start, first, size):
        def per_rows(i, carry):
            mine = pl.ds(pl.multiple_of(start + i * 16, 16), 16)
            at = pl.ds(pl.multiple_of(first + i * 16, 16), 16)
            out[mine, :] = (
                g[0, at, :].astype(F32) + gfl[at, :].astype(F32) + gfr[at, :].astype(F32)
            ).astype(BF16)
            return carry

        lax.fori_loop(0, size // 16, per_rows, 0)

    left_here(w.at[pl.ds(0, 2)], 0)
    left_here(send.at[pl.ds(1, 7)], 1)
    left_here(w.at[0], 2)
    left_here(x.at[0], 3)
    left_here(x.at[0, pl.ds(0, 2)], 4)
    left_here(part.at[pl.ds(0, 384)], 5)
    left_here(ret.at[pl.ds(CAP, 7 * CAP)], 6)
    plain_l.wait_recv()
    plain_r.wait_recv()
    summed[0].wait_recv()
    grad_end(gg_out, 0, 0, HID)
    summed[2].wait_recv()
    grad_end(gu_out, 48, 144, 48)
    grad_end(gd_out, 0, 192, 48)
    summed[1].wait_recv()
    grad_end(gu_out, 0, 96, 48)
    summed[3].wait_recv()
    grad_end(gd_out, 48, 240, 48)
    left_here(g.at[pl.ds(0, 3)], 7)


def hand_over(*refs):
    copies = []
    for i in range(4):
        rows = refs[i].shape[0] // 2
        for j in range(2):
            part = pl.ds(j * rows, rows)
            copies.append(pltpu.make_async_copy(refs[i].at[part], refs[4 + i].at[part], refs[8].at[2 * i + j]))
    for copy in copies:
        copy.start()
    for copy in copies:
        copy.wait()


def on_device(
    tokens, norm_gain, routes, route_weight, gate_weight, up_weight, down_weight, cotangent
):
    any_spec = pl.BlockSpec(memory_space=pl.ANY)
    vmem_spec = pl.BlockSpec(memory_space=pltpu.VMEM)
    rows = lambda n, t=BF16: pltpu.VMEM((n, D), t)
    outs = pl.pallas_call(
        kernel,
        out_shape=(
            pltpu.VMEM((TOK, D), BF16),
            pltpu.VMEM((HID, D), BF16),
            pltpu.VMEM((HID, D), BF16),
            pltpu.VMEM((HID, D), BF16),
        ),
        in_specs=[any_spec] * 8,
        out_specs=(vmem_spec,) * 4,
        scratch_shapes=[
            pltpu.VMEM((1, D), F32), pltpu.VMEM((1, TOK), jnp.int32), pltpu.VMEM((1, TOK), F32),
            rows(TOK), rows(TOK), rows(TOK), rows(TOK),
            pltpu.VMEM((8, 2, CAP, D), BF16),
            pltpu.VMEM((TOK, TOK), BF16), pltpu.VMEM((TOK, TOK), BF16),
            pltpu.VMEM((TOK, TOK), F32), pltpu.VMEM((TOK, 128), F32),
            pltpu.VMEM((2, SLOTS, 2, HALF, D), BF16), pltpu.VMEM((SLOTS, 3 * HID, D), BF16),
            pltpu.VMEM((768, 256), F32), pltpu.VMEM((384, 256), F32),
            pltpu.VMEM((768, 512), BF16), pltpu.VMEM((256, 768), BF16), pltpu.VMEM((384, 512), BF16),
            rows(512), rows(64), rows(64), rows(128), rows(128),
            rows(TOK), rows(TOK), rows(TOK, F32),
            pltpu.VMEM((SLOTS, 3 * HID, D), BF16), rows(144), rows(144), rows(288), rows(288),
            pltpu.SemaphoreType.DMA((N_SEND,)),
            pltpu.SemaphoreType.DMA((N_RECV,)),
            pltpu.SemaphoreType.DMA((N_LOCAL,)),
        ],
        compiler_params=pltpu.CompilerParams(
            collective_id=0, has_side_effects=True, vmem_limit_bytes=56 * 2**20
        ),
        cost_estimate=pl.CostEstimate(flops=13 * 10**9, bytes_accessed=9 * 2**20, transcendentals=2**18),
        name="learner_step",
    )(
        tokens, cotangent, norm_gain.reshape(1, D), routes.reshape(1, TOK), route_weight.reshape(1, TOK),
        gate_weight[0], up_weight[0], down_weight[0],
    )
    outs = pl.pallas_call(
        hand_over,
        out_shape=tuple(jax.ShapeDtypeStruct(out.shape, out.dtype) for out in outs),
        in_specs=[vmem_spec] * 4,
        out_specs=(any_spec,) * 4,
        scratch_shapes=[pltpu.SemaphoreType.DMA((8,))],
        name="hand_over",
    )(*(pltpu.with_memory_space_constraint(out, pltpu.VMEM) for out in outs))
    return (outs[0], outs[1][None], outs[2][None], outs[3][None])


def solution(mesh):
    token_spec = P(("dp", "expert"), None)
    weight_spec = P("dp", "expert", None)
    return jax.shard_map(
        on_device,
        mesh=mesh,
        in_specs=(token_spec, P(), token_spec, token_spec, weight_spec, weight_spec, weight_spec, token_spec),
        out_specs=(token_spec, weight_spec, weight_spec, weight_spec),
        check_vma=False,
    )
```
